32 devices in a mesh: group: 2 (over x), frame: 16 (over z, y, core).
Axes of the slice: x: 2, y: 2, z: 4, core: 2. Of those that a mesh axis runs over, the one named last changes fastest.
Arguments:
- inputs: bfloat16 [12288, 1024], P(('group', 'frame')), parts along dimension 0, may hold values from -40 to 40
- grads_out: bfloat16 [12288, 1024], P(('group', 'frame')), parts along dimension 0, may hold values from -40 to 40
- owners: int32 [8], P('group'), parts along dimension 0, may hold values from 0 to 3, each once
Outputs:
- precond: bfloat16 [8, 512, 512], P('group'), parts along dimension 0
- roots: float32 [8192, 512], P(('group', 'frame')), parts along dimension 0
The draws below stay inside these ranges and needn't reach their ends.
There are 2 independent parts, one for each index of `group`. The reference program is written for one: setup_inputs(seed, part) draws one part's arguments, and reference() takes and returns one part's arrays. A program takes and returns all parts, laid end to end along the dimension named above; each array names one. Nothing has to cross between parts.
Inputs may be any that keep to these rules, and one draw needn't show every extreme that they name: `owners`: each slot is named by exactly one block.
All inputs are finite; a program needn't handle non-finite values.
Results may differ from the reference program's by a relative error of at most 0.001.
Values may be sent and summed in bfloat16 or wider, within the bound.
A program may use at most 128 MiB of HBM per device.

```python
import math
import jax
import jax.numpy as jnp
from jax import lax

BLOCK = 512
ITERS = 3
NB = 4
DIN = 1024
COLS = 1024
TOKENS = 6144


def column_scales(key, cols):
    return jnp.exp(jax.random.uniform(key, (1, cols), jnp.float32) * math.log(10.0))


def draw_inputs(key, part):
    key = jax.random.fold_in(key, 11)
    key_col, key_val = jax.random.split(key, 2)
    spread = column_scales(key_col, DIN)
    base = jnp.clip(jax.random.normal(key_val, (TOKENS, DIN), jnp.float32), -4.0, 4.0)
    return (base * spread).astype(jnp.bfloat16)


def draw_grads_out(key, part):
    key = jax.random.fold_in(key, 12)
    key_col, key_val = jax.random.split(key, 2)
    spread = column_scales(key_col, COLS)
    base = jnp.clip(jax.random.normal(key_val, (TOKENS, COLS), jnp.float32), -4.0, 4.0)
    return (base * spread).astype(jnp.bfloat16)


def setup_inputs(seed: int = 0, part: int = 0) -> dict:
    key_of = jax.random.split(jax.random.key(seed), 4)
    part_keys = jax.random.split(jax.random.fold_in(key_of[3], part), 4)
    return {
        "inputs": draw_inputs(jax.random.fold_in(jax.random.fold_in(key_of[3], part), 71), part),
        "grads_out": draw_grads_out(jax.random.fold_in(jax.random.fold_in(key_of[3], part), 71), part),
        "owners": jax.random.permutation(part_keys[2], NB).astype(jnp.int32),
    }


damping = 0.1

def exact_dot(first_op, second_op):
    return jnp.dot(first_op, second_op, precision=lax.Precision.HIGHEST, preferred_element_type=jnp.float32)

def inverse_root(statistic):
    size_rows = statistic.shape[0]
    identity = jnp.eye(size_rows, dtype=jnp.float32)
    damped = statistic + damping * jnp.trace(statistic) / size_rows * identity
    frob_norm = jnp.sqrt(jnp.sum(damped * damped))
    zeta_scale = 5.0 / (2.0 * frob_norm)
    root_full = zeta_scale ** 0.25 * identity
    matrix = zeta_scale * damped
    for iteration in range(ITERS):
        factor_step = (5.0 * identity - matrix) * 0.25
        root_full = exact_dot(root_full, factor_step)
        square = exact_dot(factor_step, factor_step)
        matrix = exact_dot(exact_dot(square, square), matrix)
    return root_full

def reference(inputs, grads_out, owners):
    token_scale = inputs.shape[0] ** (-0.5)

    def one_block(block_id):
        x_cols = lax.dynamic_slice_in_dim(inputs, block_id % 2 * BLOCK, BLOCK, 1)
        y_cols = lax.dynamic_slice_in_dim(grads_out, block_id // 2 * BLOCK, BLOCK, 1)
        gradient = jnp.dot(x_cols.T, y_cols, preferred_element_type=jnp.float32) * token_scale
        left_root = inverse_root(exact_dot(gradient, gradient.T) / BLOCK)
        right_root = inverse_root(exact_dot(gradient.T, gradient) / BLOCK)
        precon = exact_dot(exact_dot(left_root, gradient), right_root).astype(jnp.bfloat16)
        return (precon, left_root, right_root)
    precond, left_all, right_all = lax.map(one_block, jnp.arange(NB, dtype=jnp.int32))
    inverse = jnp.argsort(owners).astype(jnp.int32)
    roots = jnp.stack([left_all[inverse], right_all[inverse]], axis=1).reshape(2 * NB * BLOCK, BLOCK)
    return (precond, roots)
```

```python
import functools

import jax
import jax.numpy as jnp
from jax import lax
from jax.experimental import pallas as pl
from jax.experimental.pallas import tpu as pltpu
from jax.sharding import PartitionSpec as P

BLOCK = 512
ITERS = 3


damping = 0.1


def partner_2(value, axis, stride):
    mask = 2**stride
    pairs = [(source, source ^ mask) for source in range(lax.axis_size(axis))]
    return lax.ppermute(value, axis, pairs)


def exact_dot(first_op, second_op):
    return jnp.dot(
        first_op, second_op, precision=lax.Precision.HIGHEST, preferred_element_type=jnp.float32
    )


def joined(own_part, other_part, own_first):
    return jnp.where(
        own_first,
        jnp.concatenate([own_part, other_part], 0),
        jnp.concatenate([other_part, own_part], 0),
    )


def body_general(inputs, grads_out, owners):
    frames = lax.axis_size("frame")
    blocks = frames // 4
    block_width = BLOCK
    quarter = block_width // 4
    half_rows = block_width // 2
    device_index = lax.axis_index("frame")
    quad_role = device_index % 4
    factor_side = quad_role // 2
    half_side = quad_role % 2
    token_scale = (inputs.shape[0] * frames) ** (-0.5)
    positions = jnp.arange(blocks, dtype=jnp.int32)
    inverse = jnp.sum(
        jnp.where(owners[None, :] == positions[:, None], positions[None, :], 0), axis=1
    )

    def block_product(block_id, row_offset, row_count):
        x_cols = lax.dynamic_slice_in_dim(
            inputs, block_id % 2 * block_width + row_offset, row_count, 1
        )
        y_cols = lax.dynamic_slice_in_dim(grads_out, block_id // 2 * block_width, block_width, 1)
        return (
            jnp.einsum("tk,tc->kc", x_cols, y_cols, preferred_element_type=jnp.float32)
            * token_scale
        )

    def one_slot(offset):
        return block_product(inverse[offset], 0, block_width)

    stacked = lax.map(
        one_slot, jnp.arange(lax.axis_size("frame") * quarter // block_width, dtype=jnp.int32)
    )
    own_part = lax.psum_scatter(
        stacked.reshape(lax.axis_size("frame") * quarter, block_width),
        "frame",
        scatter_dimension=0,
        tiled=True,
    )
    partner = partner_2(own_part, "frame", 0)
    pair_rows = joined(own_part, partner, half_side == 0)
    across = partner_2(pair_rows, "frame", 1)
    gradient = joined(pair_rows, across, factor_side == 0)
    operand = jnp.where(factor_side == 0, gradient, gradient.T)
    statistic = exact_dot(operand, operand.T) / block_width
    identity = jnp.eye(block_width, dtype=jnp.float32)
    damped = statistic + damping * jnp.trace(statistic) / block_width * identity
    frob_norm = jnp.sqrt(jnp.sum(damped * damped))
    zeta_scale = 5.0 / (2.0 * frob_norm)
    matrix = zeta_scale * damped
    root_full = zeta_scale**0.25 * identity
    for iteration in range(ITERS):
        factor_step = (5.0 * identity - matrix) * 0.25
        root_full = exact_dot(root_full, factor_step)
        square = exact_dot(factor_step, factor_step)
        matrix = exact_dot(exact_dot(square, square), matrix)
    roots_rows = lax.dynamic_slice_in_dim(root_full, half_side * half_rows, half_rows, 0)
    root_peer = partner_2(root_full, "frame", 1)
    left_root = jnp.where(factor_side == 0, root_full, root_peer)
    right_root = jnp.where(factor_side == 0, root_peer, root_full)
    left_rows = lax.dynamic_slice_in_dim(left_root, quad_role * quarter, quarter, 0)
    precond_rows = exact_dot(exact_dot(left_rows, gradient), right_root).astype(jnp.bfloat16)
    gathered = lax.all_gather(precond_rows, "frame", axis=0, tiled=True)
    gathered = gathered.reshape(blocks, block_width, block_width)
    precond = jnp.take(gathered, owners, axis=0)
    return (precond, roots_rows)


def halves(value):
    high = value.astype(jnp.bfloat16)
    low = (value - high.astype(jnp.float32)).astype(jnp.bfloat16)
    return high, low


def dot_halves(first, second, dims=((1,), (0,))):
    def one(a, b):
        return lax.dot_general(a, b, (dims, ((), ())), preferred_element_type=jnp.float32)

    return one(first[0], second[0]) + (one(first[0], second[1]) + one(first[1], second[0]))


def inverse_root(operand):
    size = operand.shape[0]
    parts = halves(operand)
    statistic = dot_halves(parts, parts, ((1,), (1,))) / size
    row = lax.broadcasted_iota(jnp.int32, (size, size), 0)
    col = lax.broadcasted_iota(jnp.int32, (size, size), 1)
    diagonal = row == col
    trace = jnp.sum(jnp.where(diagonal, statistic, 0.0))
    damped = statistic + jnp.where(diagonal, damping * trace / size, 0.0)
    zeta = 5.0 / (2.0 * jnp.sqrt(jnp.full((1, 1), jnp.sum(damped * damped), jnp.float32)))
    matrix = zeta * damped
    a = 1.25
    scale = 1.0
    deviation = None
    for iteration in range(ITERS):
        step = matrix * -0.25
        step_parts = halves(step)
        if deviation is None:
            deviation, scale = step, a
        else:
            deviation = scale * step + a * deviation + dot_halves(halves(deviation), step_parts)
            scale = scale * a
        if iteration < ITERS - 1:
            square = 2.0 * a * step + dot_halves(step_parts, step_parts)
            square_parts = halves(square)
            fourth = 2.0 * a * a * square + dot_halves(square_parts, square_parts)
            matrix = a**4 * matrix + dot_halves(halves(fourth), halves(matrix))
    root_scale = jnp.sqrt(jnp.sqrt(zeta))
    return root_scale * (deviation + jnp.where(diagonal, scale, 0.0))


def kernel(
    token_scale, owners_ref, x_ref, y_ref, out_ref, roots_ref,
    xt, part, from_core, y_sum, from_y, z_sum, from_z, grad, root_own, root_peer, rows_all,
    send_sem, recv_sem,
):
    me = lax.axis_index("frame")
    z, role = me // 4, me % 4
    y, core = role // 2, role % 2
    core_peer = me + 1 - 2 * core
    y_peer = me + 2 - 4 * y
    role_y = role + 2 - 4 * y
    planes = [((z + d) % 4) * 4 + role for d in range(4)]
    quarter, width = grad.shape[1], grad.shape[2]
    copies = []

    def copy(src, dst, target):
        index = len(copies)
        made = pltpu.make_async_remote_copy(
            src_ref=src,
            dst_ref=dst,
            send_sem=send_sem.at[index],
            recv_sem=recv_sem.at[index],
            device_id={"frame": target},
            device_id_type=pl.DeviceIdType.MESH,
        )
        made.start()
        copies.append(made)
        return made

    barrier = pltpu.get_barrier_semaphore()
    partners = [core_peer, y_peer] + planes[1:]
    for partner in partners:
        pl.semaphore_signal(
            barrier, inc=1, device_id={"frame": partner}, device_id_type=pl.DeviceIdType.MESH
        )

    xt[...] = x_ref[...].T

    def compute(d):
        slot = (z + d) % 4
        row_bit, col_bit = jnp.int32(0), jnp.int32(0)
        for b in range(1, 4):
            here = (owners_ref[b] == slot).astype(jnp.int32)
            row_bit, col_bit = row_bit + here * (b % 2), col_bit + here * (b // 2)
        x_rows = jnp.where(
            jnp.full((width, x_ref.shape[0]), row_bit) == 0, xt[:width, :], xt[width:, :]
        )
        y_cols = jnp.where(
            jnp.full((x_ref.shape[0], width), col_bit) == 0, y_ref[:, :width], y_ref[:, width:]
        )
        part[d] = jnp.dot(x_rows, y_cols, preferred_element_type=jnp.float32).reshape(
            4, quarter, width
        )

    def to_core(d):
        return [
            copy(
                part.at[d, 2 * side + 1 - core], from_core.at[d, index], core_peer
            )
            for index, side in enumerate((1 - y, y))
        ]

    def to_y(d, sent):
        sent[0].wait_recv()
        y_sum[d] = part[d, 2 * (1 - y) + core] + from_core[d, 0]
        return copy(y_sum.at[d], from_y.at[d], y_peer)

    order = (2, 1, 3, 0)
    core_copies, y_copies, z_copies = {}, {}, {}
    for index, d in enumerate(order):
        compute(d)
        if index == 0:
            pl.semaphore_wait(barrier, len(partners))
        core_copies[d] = to_core(d)
        if index > 0:
            before = order[index - 1]
            y_copies[before] = to_y(before, core_copies[before])
    y_copies[0] = to_y(0, core_copies[0])
    for d in order:
        core_copies[d][1].wait_recv()
        y_copies[d].wait_recv()
        z_sum[d] = part[d, role] + from_core[d, 1] + from_y[d]
        if d > 0:
            z_copies[d] = copy(z_sum.at[d], from_z.at[d - 1], planes[d])
    total = z_sum[0]
    for d in order[:3]:
        z_copies[d].wait_recv()
        total = total + from_z[d - 1]
    grad[role] = total * token_scale
    own_core = copy(grad.at[role], grad.at[role], core_peer)
    own_y = copy(grad.at[role], grad.at[role], y_peer)
    own_y.wait_recv()
    forward = copy(grad.at[role_y], grad.at[role_y], core_peer)
    own_core.wait_recv()
    forward.wait_recv()

    gradient = grad[...].reshape(4 * quarter, width)
    root_own[...] = inverse_root(jnp.where(core == 0, gradient, gradient.T))
    exchange = copy(root_own, root_peer, core_peer)
    exchange.wait_recv()

    half = pl.ds(pl.multiple_of(core * 2 * quarter, 2 * quarter), 2 * quarter)
    roots_ref[...] = jnp.where(y == core, root_own[half, :], root_peer[half, :])
    mine = pl.ds(pl.multiple_of(role * quarter, quarter), quarter)
    left = jnp.where(core == 0, root_own[mine, :], root_peer[mine, :])
    right = jnp.where(core == 0, root_peer[...], root_own[...])
    product = dot_halves(halves(left), halves(grad[...].reshape(4 * quarter, width)))
    rows_all[z, role] = dot_halves(halves(product), halves(right)).astype(jnp.bfloat16)

    def spread(plane, which, target):
        place = rows_all.at[plane, which]
        return copy(place, place, target)

    z_rows = {d: spread(z, role, planes[d]) for d in (2, 1, 3)}
    y_rows = {0: spread(z, role, y_peer)}
    core_rows = [spread(z, role, core_peer)]
    for d in (1, 3, 2):
        z_rows[d].wait_recv()
        plane = (z + 4 - d) % 4
        y_rows[d] = spread(plane, role, y_peer)
        core_rows.append(spread(plane, role, core_peer))
    for d in (0, 1, 3, 2):
        y_rows[d].wait_recv()
        core_rows.append(spread((z + 4 - d) % 4, role_y, core_peer))
    for made in core_rows:
        made.wait_recv()
    for b in range(4):
        out_ref[b] = rows_all[owners_ref[b]].reshape(4 * quarter, width)
    for made in copies:
        made.wait_send()


def body(inputs, grads_out, owners):
    frames = lax.axis_size("frame")
    quarter = BLOCK // 4
    messages = 8 + 4 + 3 + 3 + 1 + 3 + 4 + 4 + 4
    f32 = jnp.float32
    return pl.pallas_call(
        functools.partial(kernel, (inputs.shape[0] * frames) ** (-0.5)),
        out_shape=(
            jax.ShapeDtypeStruct((4, BLOCK, BLOCK), jnp.bfloat16),
            jax.ShapeDtypeStruct((2 * quarter, BLOCK), f32),
        ),
        in_specs=[
            pl.BlockSpec(memory_space=pltpu.SMEM),
            pl.BlockSpec(memory_space=pltpu.VMEM),
            pl.BlockSpec(memory_space=pltpu.VMEM),
        ],
        out_specs=(
            pl.BlockSpec(memory_space=pltpu.VMEM),
            pl.BlockSpec(memory_space=pltpu.VMEM),
        ),
        scratch_shapes=[
            pltpu.VMEM((inputs.shape[1], inputs.shape[0]), jnp.bfloat16),
            pltpu.VMEM((4, 4, quarter, BLOCK), f32),
            pltpu.VMEM((4, 2, quarter, BLOCK), f32),
            pltpu.VMEM((4, quarter, BLOCK), f32),
            pltpu.VMEM((4, quarter, BLOCK), f32),
            pltpu.VMEM((4, quarter, BLOCK), f32),
            pltpu.VMEM((3, quarter, BLOCK), f32),
            pltpu.VMEM((4, quarter, BLOCK), f32),
            pltpu.VMEM((BLOCK, BLOCK), f32),
            pltpu.VMEM((BLOCK, BLOCK), f32),
            pltpu.VMEM((4, 4, quarter, BLOCK), jnp.bfloat16),
            pltpu.SemaphoreType.DMA((messages,)),
            pltpu.SemaphoreType.DMA((messages,)),
        ],
        compiler_params=pltpu.CompilerParams(
            collective_id=0, has_side_effects=True, vmem_limit_bytes=56 * 2**20
        ),
    )(owners, inputs, grads_out)


def solution(mesh):
    in_specs = (P(("group", "frame"), None), P(("group", "frame"), None), P("group"))
    out_specs = (P("group", None, None), P(("group", "frame"), None))
    fused = mesh.shape["frame"] == 16
    return jax.shard_map(
        body if fused else body_general,
        mesh=mesh,
        in_specs=in_specs,
        out_specs=out_specs,
        check_vma=False,
    )
```

```python
import functools

import jax
import jax.numpy as jnp
from jax import lax
from jax.experimental import pallas as pl
from jax.experimental.pallas import tpu as pltpu
from jax.sharding import PartitionSpec as P

BLOCK = 512
ITERS = 3


damping = 0.1


def partner_2(value, axis, stride):
    mask = 2**stride
    pairs = [(source, source ^ mask) for source in range(lax.axis_size(axis))]
    return lax.ppermute(value, axis, pairs)


def exact_dot(first_op, second_op):
    return jnp.dot(
        first_op, second_op, precision=lax.Precision.HIGHEST, preferred_element_type=jnp.float32
    )


def joined(own_part, other_part, own_first):
    return jnp.where(
        own_first,
        jnp.concatenate([own_part, other_part], 0),
        jnp.concatenate([other_part, own_part], 0),
    )


def body_general(inputs, grads_out, owners):
    frames = lax.axis_size("frame")
    blocks = frames // 4
    block_width = BLOCK
    quarter = block_width // 4
    half_rows = block_width // 2
    device_index = lax.axis_index("frame")
    quad_role = device_index % 4
    factor_side = quad_role // 2
    half_side = quad_role % 2
    token_scale = (inputs.shape[0] * frames) ** (-0.5)
    positions = jnp.arange(blocks, dtype=jnp.int32)
    inverse = jnp.sum(
        jnp.where(owners[None, :] == positions[:, None], positions[None, :], 0), axis=1
    )

    def block_product(block_id, row_offset, row_count):
        x_cols = lax.dynamic_slice_in_dim(
            inputs, block_id % 2 * block_width + row_offset, row_count, 1
        )
        y_cols = lax.dynamic_slice_in_dim(grads_out, block_id // 2 * block_width, block_width, 1)
        return (
            jnp.einsum("tk,tc->kc", x_cols, y_cols, preferred_element_type=jnp.float32)
            * token_scale
        )

    def one_slot(offset):
        return block_product(inverse[offset], 0, block_width)

    stacked = lax.map(
        one_slot, jnp.arange(lax.axis_size("frame") * quarter // block_width, dtype=jnp.int32)
    )
    own_part = lax.psum_scatter(
        stacked.reshape(lax.axis_size("frame") * quarter, block_width),
        "frame",
        scatter_dimension=0,
        tiled=True,
    )
    partner = partner_2(own_part, "frame", 0)
    pair_rows = joined(own_part, partner, half_side == 0)
    across = partner_2(pair_rows, "frame", 1)
    gradient = joined(pair_rows, across, factor_side == 0)
    operand = jnp.where(factor_side == 0, gradient, gradient.T)
    statistic = exact_dot(operand, operand.T) / block_width
    identity = jnp.eye(block_width, dtype=jnp.float32)
    damped = statistic + damping * jnp.trace(statistic) / block_width * identity
    frob_norm = jnp.sqrt(jnp.sum(damped * damped))
    zeta_scale = 5.0 / (2.0 * frob_norm)
    matrix = zeta_scale * damped
    root_full = zeta_scale**0.25 * identity
    for iteration in range(ITERS):
        factor_step = (5.0 * identity - matrix) * 0.25
        root_full = exact_dot(root_full, factor_step)
        square = exact_dot(factor_step, factor_step)
        matrix = exact_dot(exact_dot(square, square), matrix)
    roots_rows = lax.dynamic_slice_in_dim(root_full, half_side * half_rows, half_rows, 0)
    root_peer = partner_2(root_full, "frame", 1)
    left_root = jnp.where(factor_side == 0, root_full, root_peer)
    right_root = jnp.where(factor_side == 0, root_peer, root_full)
    left_rows = lax.dynamic_slice_in_dim(left_root, quad_role * quarter, quarter, 0)
    precond_rows = exact_dot(exact_dot(left_rows, gradient), right_root).astype(jnp.bfloat16)
    gathered = lax.all_gather(precond_rows, "frame", axis=0, tiled=True)
    gathered = gathered.reshape(blocks, block_width, block_width)
    precond = jnp.take(gathered, owners, axis=0)
    return (precond, roots_rows)


def halves(value):
    high = value.astype(jnp.bfloat16)
    low = (value - high.astype(jnp.float32)).astype(jnp.bfloat16)
    return high, low


def dot_halves(first, second, dims=((1,), (0,))):
    def one(a, b):
        return lax.dot_general(a, b, (dims, ((), ())), preferred_element_type=jnp.float32)

    return one(first[0], second[0]) + (one(first[0], second[1]) + one(first[1], second[0]))


def inverse_root(operand):
    size = operand.shape[0]
    parts = halves(operand)
    statistic = dot_halves(parts, parts, ((1,), (1,))) / size
    row = lax.broadcasted_iota(jnp.int32, (size, size), 0)
    col = lax.broadcasted_iota(jnp.int32, (size, size), 1)
    diagonal = row == col
    trace = jnp.sum(jnp.where(diagonal, statistic, 0.0))
    damped = statistic + jnp.where(diagonal, damping * trace / size, 0.0)
    zeta = 5.0 / (2.0 * jnp.sqrt(jnp.full((1, 1), jnp.sum(damped * damped), jnp.float32)))
    matrix = zeta * damped
    a = 1.25
    scale = 1.0
    deviation = None
    for iteration in range(ITERS):
        step = matrix * -0.25
        step_parts = halves(step)
        if deviation is None:
            deviation, scale = step, a
        else:
            deviation = scale * step + a * deviation + dot_halves(halves(deviation), step_parts)
            scale = scale * a
        if iteration < ITERS - 1:
            square = 2.0 * a * step + dot_halves(step_parts, step_parts)
            square_parts = halves(square)
            fourth = 2.0 * a * a * square + dot_halves(square_parts, square_parts)
            matrix = a**4 * matrix + dot_halves(halves(fourth), halves(matrix))
    root_scale = jnp.sqrt(jnp.sqrt(zeta))
    return root_scale * (deviation + jnp.where(diagonal, scale, 0.0))


def kernel(
    token_scale, owners_ref, x_ref, y_ref, out_ref, roots_ref,
    xt, part, from_core, y_sum, from_y, z_sum, from_z, grad, root_own, root_peer, rows_all,
    send_sem, recv_sem,
):
    me = lax.axis_index("frame")
    z, role = me // 4, me % 4
    y, core = role // 2, role % 2
    core_peer = me + 1 - 2 * core
    y_peer = me + 2 - 4 * y
    role_y = role + 2 - 4 * y
    planes = [((z + d) % 4) * 4 + role for d in range(4)]
    quarter, width = grad.shape[1], grad.shape[2]
    copies = []

    def copy(src, dst, target):
        index = len(copies)
        made = pltpu.make_async_remote_copy(
            src_ref=src,
            dst_ref=dst,
            send_sem=send_sem.at[index],
            recv_sem=recv_sem.at[index],
            device_id={"frame": target},
            device_id_type=pl.DeviceIdType.MESH,
        )
        made.start()
        copies.append(made)
        return made

    barrier = pltpu.get_barrier_semaphore()
    partners = [core_peer, y_peer] + planes[1:]
    for partner in partners:
        pl.semaphore_signal(
            barrier, inc=1, device_id={"frame": partner}, device_id_type=pl.DeviceIdType.MESH
        )

    half_width = width // 2
    for side in (1 - y, y):
        for bit in range(2):
            cols = pl.ds(pl.multiple_of(bit * width + side * half_width, half_width), half_width)
            xt[2 * bit + side] = x_ref[:, cols].T

    def compute(d, side):
        slot = (z + d) % 4
        row_bit, col_bit = jnp.int32(0), jnp.int32(0)
        for b in range(1, 4):
            here = (owners_ref[b] == slot).astype(jnp.int32)
            row_bit, col_bit = row_bit + here * (b % 2), col_bit + here * (b // 2)
        x_rows = jnp.where(
            jnp.full((half_width, x_ref.shape[0]), row_bit) == 0, xt[side], xt[2 + side]
        )
        y_cols = jnp.where(
            jnp.full((x_ref.shape[0], width), col_bit) == 0, y_ref[:, :width], y_ref[:, width:]
        )
        product = jnp.dot(x_rows, y_cols, preferred_element_type=jnp.float32)
        part[d, 2 * side] = product[:quarter]
        part[d, 2 * side + 1] = product[quarter:]

    def to_core(d, side, index):
        return copy(part.at[d, 2 * side + 1 - core], from_core.at[d, index], core_peer)

    def to_y(d, sent):
        sent.wait_recv()
        y_sum[d] = part[d, 2 * (1 - y) + core] + from_core[d, 0]
        return copy(y_sum.at[d], from_y.at[d], y_peer)

    order = (2, 1, 3, 0)
    away, kept, y_copies, z_copies = {}, {}, {}, {}
    for index, d in enumerate(order):
        compute(d, 1 - y)
        if index == 0:
            pl.semaphore_wait(barrier, len(partners))
        away[d] = to_core(d, 1 - y, 0)
        if index > 0:
            before = order[index - 1]
            y_copies[before] = to_y(before, away[before])
    y_copies[0] = to_y(0, away[0])
    for d in order:
        compute(d, y)
        kept[d] = to_core(d, y, 1)
    for d in order:
        kept[d].wait_recv()
        y_copies[d].wait_recv()
        z_sum[d] = part[d, role] + from_core[d, 1] + from_y[d]
        if d > 0:
            z_copies[d] = copy(z_sum.at[d], from_z.at[d - 1], planes[d])
    total = z_sum[0]
    for d in order[:3]:
        z_copies[d].wait_recv()
        total = total + from_z[d - 1]
    grad[role] = total * token_scale
    own_core = copy(grad.at[role], grad.at[role], core_peer)
    own_y = copy(grad.at[role], grad.at[role], y_peer)
    own_y.wait_recv()
    forward = copy(grad.at[role_y], grad.at[role_y], core_peer)
    own_core.wait_recv()
    forward.wait_recv()

    gradient = grad[...].reshape(4 * quarter, width)
    root_own[...] = inverse_root(jnp.where(core == 0, gradient, gradient.T))
    exchange = copy(root_own, root_peer, core_peer)
    exchange.wait_recv()

    half = pl.ds(pl.multiple_of(core * 2 * quarter, 2 * quarter), 2 * quarter)
    roots_ref[...] = jnp.where(y == core, root_own[half, :], root_peer[half, :])
    mine = pl.ds(pl.multiple_of(role * quarter, quarter), quarter)
    left = jnp.where(core == 0, root_own[mine, :], root_peer[mine, :])
    right = jnp.where(core == 0, root_peer[...], root_own[...])
    product = dot_halves(halves(left), halves(grad[...].reshape(4 * quarter, width)))
    rows_all[z, role] = dot_halves(halves(product), halves(right)).astype(jnp.bfloat16)

    base = len(copies)
    up, down, over, near, passed = base, base + 3, base + 6, base + 10, base + 14
    above, below = planes[1], planes[3]

    def rows_copy(index, plane, which, target):
        place = rows_all.at[plane, which]
        return pltpu.make_async_remote_copy(
            src_ref=place,
            dst_ref=place,
            send_sem=send_sem.at[index],
            recv_sem=recv_sem.at[index],
            device_id={"frame": target},
            device_id_type=pl.DeviceIdType.MESH,
        )

    def share(plane):
        rows_copy(over + plane, plane, role, y_peer).start()
        rows_copy(near + plane, plane, role, core_peer).start()

    def along(k):
        @pl.when(z >= k)
        def _():
            rows_copy(up + k - 1, z - k, role, above).wait_recv()
            if k < 3:
                @pl.when(z < 3)
                def _():
                    rows_copy(up + k, z - k, role, above).start()
            share(z - k)

        @pl.when(z + k <= 3)
        def _():
            rows_copy(down + k - 1, z + k, role, below).wait_recv()
            if k < 3:
                @pl.when(z > 0)
                def _():
                    rows_copy(down + k, z + k, role, below).start()
            share(z + k)

    def pass_on(plane):
        rows_copy(over + plane, plane, role, y_peer).wait_recv()
        rows_copy(passed + plane, plane, role_y, core_peer).start()

    def pass_step(k):
        @pl.when(z >= k)
        def _():
            pass_on(z - k)

        @pl.when(z + k <= 3)
        def _():
            pass_on(z + k)

    @pl.when(z < 3)
    def _():
        rows_copy(up, z, role, above).start()

    @pl.when(z > 0)
    def _():
        rows_copy(down, z, role, below).start()

    share(z)
    along(1)
    pass_on(z)
    along(2)
    pass_step(1)
    along(3)
    pass_step(2)
    pass_step(3)
    for plane in range(4):
        rows_copy(near + plane, plane, role, core_peer).wait_recv()
        rows_copy(passed + plane, plane, role_y, core_peer).wait_recv()
    for b in range(4):
        out_ref[b] = rows_all[owners_ref[b]].reshape(4 * quarter, width)
    for made in copies:
        made.wait_send()
    for k in range(3):
        @pl.when((z >= k) & (z < 3))
        def _():
            rows_copy(up + k, z, role, above).wait_send()

        @pl.when((z + k <= 3) & (z > 0))
        def _():
            rows_copy(down + k, z, role, below).wait_send()

    for plane in range(4):
        rows_copy(over + plane, plane, role, y_peer).wait_send()
        rows_copy(near + plane, plane, role, core_peer).wait_send()
        rows_copy(passed + plane, plane, role_y, core_peer).wait_send()


def body(inputs, grads_out, owners):
    frames = lax.axis_size("frame")
    quarter = BLOCK // 4
    messages = 8 + 4 + 3 + 3 + 1 + 3 + 3 + 4 + 4 + 4
    f32 = jnp.float32
    return pl.pallas_call(
        functools.partial(kernel, (inputs.shape[0] * frames) ** (-0.5)),
        out_shape=(
            jax.ShapeDtypeStruct((4, BLOCK, BLOCK), jnp.bfloat16),
            jax.ShapeDtypeStruct((2 * quarter, BLOCK), f32),
        ),
        in_specs=[
            pl.BlockSpec(memory_space=pltpu.SMEM),
            pl.BlockSpec(memory_space=pltpu.VMEM),
            pl.BlockSpec(memory_space=pltpu.VMEM),
        ],
        out_specs=(
            pl.BlockSpec(memory_space=pltpu.VMEM),
            pl.BlockSpec(memory_space=pltpu.VMEM),
        ),
        scratch_shapes=[
            pltpu.VMEM((4, inputs.shape[1] // 4, inputs.shape[0]), jnp.bfloat16),
            pltpu.VMEM((4, 4, quarter, BLOCK), f32),
            pltpu.VMEM((4, 2, quarter, BLOCK), f32),
            pltpu.VMEM((4, quarter, BLOCK), f32),
            pltpu.VMEM((4, quarter, BLOCK), f32),
            pltpu.VMEM((4, quarter, BLOCK), f32),
            pltpu.VMEM((3, quarter, BLOCK), f32),
            pltpu.VMEM((4, quarter, BLOCK), f32),
            pltpu.VMEM((BLOCK, BLOCK), f32),
            pltpu.VMEM((BLOCK, BLOCK), f32),
            pltpu.VMEM((4, 4, quarter, BLOCK), jnp.bfloat16),
            pltpu.SemaphoreType.DMA((messages,)),
            pltpu.SemaphoreType.DMA((messages,)),
        ],
        compiler_params=pltpu.CompilerParams(
            collective_id=0, has_side_effects=True, vmem_limit_bytes=56 * 2**20
        ),
    )(owners, inputs, grads_out)


def solution(mesh):
    in_specs = (P(("group", "frame"), None), P(("group", "frame"), None), P("group"))
    out_specs = (P("group", None, None), P(("group", "frame"), None))
    fused = mesh.shape["frame"] == 16
    return jax.shard_map(
        body if fused else body_general,
        mesh=mesh,
        in_specs=in_specs,
        out_specs=out_specs,
        check_vma=False,
    )
```

```python
import functools

import jax
import jax.numpy as jnp
from jax import lax
from jax.experimental import pallas as pl
from jax.experimental.pallas import tpu as pltpu
from jax.sharding import PartitionSpec as P

BLOCK = 512
ITERS = 3


damping = 0.1


def partner_2(value, axis, stride):
    mask = 2**stride
    pairs = [(source, source ^ mask) for source in range(lax.axis_size(axis))]
    return lax.ppermute(value, axis, pairs)


def exact_dot(first_op, second_op):
    return jnp.dot(
        first_op, second_op, precision=lax.Precision.HIGHEST, preferred_element_type=jnp.float32
    )


def joined(own_part, other_part, own_first):
    return jnp.where(
        own_first,
        jnp.concatenate([own_part, other_part], 0),
        jnp.concatenate([other_part, own_part], 0),
    )


def body_general(inputs, grads_out, owners):
    frames = lax.axis_size("frame")
    blocks = frames // 4
    block_width = BLOCK
    quarter = block_width // 4
    half_rows = block_width // 2
    device_index = lax.axis_index("frame")
    quad_role = device_index % 4
    factor_side = quad_role // 2
    half_side = quad_role % 2
    token_scale = (inputs.shape[0] * frames) ** (-0.5)
    positions = jnp.arange(blocks, dtype=jnp.int32)
    inverse = jnp.sum(
        jnp.where(owners[None, :] == positions[:, None], positions[None, :], 0), axis=1
    )

    def block_product(block_id, row_offset, row_count):
        x_cols = lax.dynamic_slice_in_dim(
            inputs, block_id % 2 * block_width + row_offset, row_count, 1
        )
        y_cols = lax.dynamic_slice_in_dim(grads_out, block_id // 2 * block_width, block_width, 1)
        return (
            jnp.einsum("tk,tc->kc", x_cols, y_cols, preferred_element_type=jnp.float32)
            * token_scale
        )

    def one_slot(offset):
        return block_product(inverse[offset], 0, block_width)

    stacked = lax.map(
        one_slot, jnp.arange(lax.axis_size("frame") * quarter // block_width, dtype=jnp.int32)
    )
    own_part = lax.psum_scatter(
        stacked.reshape(lax.axis_size("frame") * quarter, block_width),
        "frame",
        scatter_dimension=0,
        tiled=True,
    )
    partner = partner_2(own_part, "frame", 0)
    pair_rows = joined(own_part, partner, half_side == 0)
    across = partner_2(pair_rows, "frame", 1)
    gradient = joined(pair_rows, across, factor_side == 0)
    operand = jnp.where(factor_side == 0, gradient, gradient.T)
    statistic = exact_dot(operand, operand.T) / block_width
    identity = jnp.eye(block_width, dtype=jnp.float32)
    damped = statistic + damping * jnp.trace(statistic) / block_width * identity
    frob_norm = jnp.sqrt(jnp.sum(damped * damped))
    zeta_scale = 5.0 / (2.0 * frob_norm)
    matrix = zeta_scale * damped
    root_full = zeta_scale**0.25 * identity
    for iteration in range(ITERS):
        factor_step = (5.0 * identity - matrix) * 0.25
        root_full = exact_dot(root_full, factor_step)
        square = exact_dot(factor_step, factor_step)
        matrix = exact_dot(exact_dot(square, square), matrix)
    roots_rows = lax.dynamic_slice_in_dim(root_full, half_side * half_rows, half_rows, 0)
    root_peer = partner_2(root_full, "frame", 1)
    left_root = jnp.where(factor_side == 0, root_full, root_peer)
    right_root = jnp.where(factor_side == 0, root_peer, root_full)
    left_rows = lax.dynamic_slice_in_dim(left_root, quad_role * quarter, quarter, 0)
    precond_rows = exact_dot(exact_dot(left_rows, gradient), right_root).astype(jnp.bfloat16)
    gathered = lax.all_gather(precond_rows, "frame", axis=0, tiled=True)
    gathered = gathered.reshape(blocks, block_width, block_width)
    precond = jnp.take(gathered, owners, axis=0)
    return (precond, roots_rows)


def halves(value):
    high = value.astype(jnp.bfloat16)
    low = (value - high.astype(jnp.float32)).astype(jnp.bfloat16)
    return high, low


def dot_halves(first, second, dims=((1,), (0,))):
    left = jnp.concatenate([first[0], first[1], first[0]], dims[0][0])
    right = jnp.concatenate([second[0], second[0], second[1]], dims[1][0])
    return lax.dot_general(left, right, (dims, ((), ())), preferred_element_type=jnp.float32)


def inverse_root(operand):
    size = operand.shape[0]
    parts = halves(operand)
    statistic = dot_halves(parts, parts, ((1,), (1,))) / size
    row = lax.broadcasted_iota(jnp.int32, (size, size), 0)
    col = lax.broadcasted_iota(jnp.int32, (size, size), 1)
    diagonal = row == col
    trace = jnp.sum(jnp.where(diagonal, statistic, 0.0))
    damped = statistic + jnp.where(diagonal, damping * trace / size, 0.0)
    zeta = 5.0 / (2.0 * jnp.sqrt(jnp.full((1, 1), jnp.sum(damped * damped), jnp.float32)))
    matrix = zeta * damped
    a = 1.25
    scale = 1.0
    deviation = None
    for iteration in range(ITERS):
        step = matrix * -0.25
        step_parts = halves(step)
        if deviation is None:
            deviation, scale = step, a
        else:
            deviation = scale * step + a * deviation + dot_halves(halves(deviation), step_parts)
            scale = scale * a
        if iteration < ITERS - 1:
            square = 2.0 * a * step + dot_halves(step_parts, step_parts)
            square_parts = halves(square)
            fourth = 2.0 * a * a * square + dot_halves(square_parts, square_parts)
            matrix = a**4 * matrix + dot_halves(halves(fourth), halves(matrix))
    root_scale = jnp.sqrt(jnp.sqrt(zeta))
    return root_scale * (deviation + jnp.where(diagonal, scale, 0.0))


def kernel(
    token_scale, owners_ref, x_ref, y_ref, out_ref, roots_ref,
    xt, part, from_core, y_sum, from_y, z_sum, from_z, grad, root_own, root_peer, rows_all,
    send_sem, recv_sem,
):
    me = lax.axis_index("frame")
    z, role = me // 4, me % 4
    y, core = role // 2, role % 2
    core_peer = me + 1 - 2 * core
    y_peer = me + 2 - 4 * y
    role_y = role + 2 - 4 * y
    planes = [((z + d) % 4) * 4 + role for d in range(4)]
    quarter, width = grad.shape[1], grad.shape[2]
    copies = []

    def copy(src, dst, target):
        index = len(copies)
        made = pltpu.make_async_remote_copy(
            src_ref=src,
            dst_ref=dst,
            send_sem=send_sem.at[index],
            recv_sem=recv_sem.at[index],
            device_id={"frame": target},
            device_id_type=pl.DeviceIdType.MESH,
        )
        made.start()
        copies.append(made)
        return made

    barrier = pltpu.get_barrier_semaphore()
    partners = [core_peer, y_peer] + planes[1:]
    for partner in partners:
        pl.semaphore_signal(
            barrier, inc=1, device_id={"frame": partner}, device_id_type=pl.DeviceIdType.MESH
        )

    half_width = width // 2
    for side in (1 - y, y):
        for bit in range(2):
            cols = pl.ds(pl.multiple_of(bit * width + side * half_width, half_width), half_width)
            xt[2 * bit + side] = x_ref[:, cols].T

    def compute(d, side):
        slot = (z + d) % 4
        row_bit, col_bit = jnp.int32(0), jnp.int32(0)
        for b in range(1, 4):
            here = (owners_ref[b] == slot).astype(jnp.int32)
            row_bit, col_bit = row_bit + here * (b % 2), col_bit + here * (b // 2)
        x_rows = jnp.where(
            jnp.full((half_width, x_ref.shape[0]), row_bit) == 0, xt[side], xt[2 + side]
        )
        y_cols = jnp.where(
            jnp.full((x_ref.shape[0], width), col_bit) == 0, y_ref[:, :width], y_ref[:, width:]
        )
        product = jnp.dot(x_rows, y_cols, preferred_element_type=jnp.float32)
        part[d, 2 * side] = product[:quarter]
        part[d, 2 * side + 1] = product[quarter:]

    def to_core(d, side, index):
        return copy(part.at[d, 2 * side + 1 - core], from_core.at[d, index], core_peer)

    def to_y(d, sent):
        sent.wait_recv()
        y_sum[d] = part[d, 2 * (1 - y) + core] + from_core[d, 0]
        return copy(y_sum.at[d], from_y.at[d], y_peer)

    order = (2, 1, 3, 0)
    away, kept, y_copies, z_copies = {}, {}, {}, {}
    for index, d in enumerate(order):
        compute(d, 1 - y)
        if index == 0:
            pl.semaphore_wait(barrier, len(partners))
        away[d] = to_core(d, 1 - y, 0)
        if index > 0:
            before = order[index - 1]
            y_copies[before] = to_y(before, away[before])
    y_copies[0] = to_y(0, away[0])

    def to_z(d):
        kept[d].wait_recv()
        y_copies[d].wait_recv()
        z_sum[d] = part[d, role] + from_core[d, 1] + from_y[d]
        if d > 0:
            z_copies[d] = copy(z_sum.at[d], from_z.at[d - 1], planes[d])

    for index, d in enumerate(order):
        compute(d, y)
        kept[d] = to_core(d, y, 1)
        if index > 0:
            to_z(order[index - 1])
    to_z(0)
    total = z_sum[0]
    for d in order[:3]:
        z_copies[d].wait_recv()
        total = total + from_z[d - 1]
    grad[role] = total * token_scale
    own_core = copy(grad.at[role], grad.at[role], core_peer)
    own_y = copy(grad.at[role], grad.at[role], y_peer)
    own_y.wait_recv()
    forward = copy(grad.at[role_y], grad.at[role_y], core_peer)
    own_core.wait_recv()
    forward.wait_recv()

    gradient = grad[...].reshape(4 * quarter, width)
    root_own[...] = inverse_root(jnp.where(core == 0, gradient, gradient.T))
    exchange = copy(root_own, root_peer, core_peer)
    exchange.wait_recv()

    half = pl.ds(pl.multiple_of(core * 2 * quarter, 2 * quarter), 2 * quarter)
    roots_ref[...] = jnp.where(y == core, root_own[half, :], root_peer[half, :])
    mine = pl.ds(pl.multiple_of(role * quarter, quarter), quarter)
    left = jnp.where(core == 0, root_own[mine, :], root_peer[mine, :])
    right = jnp.where(core == 0, root_peer[...], root_own[...])
    product = dot_halves(halves(left), halves(grad[...].reshape(4 * quarter, width)))
    rows_all[z, role] = dot_halves(halves(product), halves(right)).astype(jnp.bfloat16)

    base = len(copies)
    up, down, over, near, passed = base, base + 3, base + 6, base + 10, base + 14
    above, below = planes[1], planes[3]

    def rows_copy(index, plane, which, target):
        place = rows_all.at[plane, which]
        return pltpu.make_async_remote_copy(
            src_ref=place,
            dst_ref=place,
            send_sem=send_sem.at[index],
            recv_sem=recv_sem.at[index],
            device_id={"frame": target},
            device_id_type=pl.DeviceIdType.MESH,
        )

    def share(plane):
        rows_copy(over + plane, plane, role, y_peer).start()
        rows_copy(near + plane, plane, role, core_peer).start()

    def along(k):
        @pl.when(z >= k)
        def _():
            rows_copy(up + k - 1, z - k, role, above).wait_recv()
            if k < 3:
                @pl.when(z < 3)
                def _():
                    rows_copy(up + k, z - k, role, above).start()
            share(z - k)

        @pl.when(z + k <= 3)
        def _():
            rows_copy(down + k - 1, z + k, role, below).wait_recv()
            if k < 3:
                @pl.when(z > 0)
                def _():
                    rows_copy(down + k, z + k, role, below).start()
            share(z + k)

    def pass_on(plane):
        rows_copy(over + plane, plane, role, y_peer).wait_recv()
        rows_copy(passed + plane, plane, role_y, core_peer).start()

    def pass_step(k):
        @pl.when(z >= k)
        def _():
            pass_on(z - k)

        @pl.when(z + k <= 3)
        def _():
            pass_on(z + k)

    @pl.when(z < 3)
    def _():
        rows_copy(up, z, role, above).start()

    @pl.when(z > 0)
    def _():
        rows_copy(down, z, role, below).start()

    share(z)
    along(1)
    pass_on(z)
    along(2)
    pass_step(1)
    along(3)
    pass_step(2)
    pass_step(3)
    for plane in range(4):
        rows_copy(near + plane, plane, role, core_peer).wait_recv()
        rows_copy(passed + plane, plane, role_y, core_peer).wait_recv()
    for b in range(4):
        out_ref[b] = rows_all[owners_ref[b]].reshape(4 * quarter, width)
    for made in copies:
        made.wait_send()
    for k in range(3):
        @pl.when((z >= k) & (z < 3))
        def _():
            rows_copy(up + k, z, role, above).wait_send()

        @pl.when((z + k <= 3) & (z > 0))
        def _():
            rows_copy(down + k, z, role, below).wait_send()

    for plane in range(4):
        rows_copy(over + plane, plane, role, y_peer).wait_send()
        rows_copy(near + plane, plane, role, core_peer).wait_send()
        rows_copy(passed + plane, plane, role_y, core_peer).wait_send()


def body(inputs, grads_out, owners):
    frames = lax.axis_size("frame")
    quarter = BLOCK // 4
    messages = 8 + 4 + 3 + 3 + 1 + 3 + 3 + 4 + 4 + 4
    f32 = jnp.float32
    return pl.pallas_call(
        functools.partial(kernel, (inputs.shape[0] * frames) ** (-0.5)),
        out_shape=(
            jax.ShapeDtypeStruct((4, BLOCK, BLOCK), jnp.bfloat16),
            jax.ShapeDtypeStruct((2 * quarter, BLOCK), f32),
        ),
        in_specs=[
            pl.BlockSpec(memory_space=pltpu.SMEM),
            pl.BlockSpec(memory_space=pltpu.VMEM),
            pl.BlockSpec(memory_space=pltpu.VMEM),
        ],
        out_specs=(
            pl.BlockSpec(memory_space=pltpu.VMEM),
            pl.BlockSpec(memory_space=pltpu.VMEM),
        ),
        scratch_shapes=[
            pltpu.VMEM((4, inputs.shape[1] // 4, inputs.shape[0]), jnp.bfloat16),
            pltpu.VMEM((4, 4, quarter, BLOCK), f32),
            pltpu.VMEM((4, 2, quarter, BLOCK), f32),
            pltpu.VMEM((4, quarter, BLOCK), f32),
            pltpu.VMEM((4, quarter, BLOCK), f32),
            pltpu.VMEM((4, quarter, BLOCK), f32),
            pltpu.VMEM((3, quarter, BLOCK), f32),
            pltpu.VMEM((4, quarter, BLOCK), f32),
            pltpu.VMEM((BLOCK, BLOCK), f32),
            pltpu.VMEM((BLOCK, BLOCK), f32),
            pltpu.VMEM((4, 4, quarter, BLOCK), jnp.bfloat16),
            pltpu.SemaphoreType.DMA((messages,)),
            pltpu.SemaphoreType.DMA((messages,)),
        ],
        compiler_params=pltpu.CompilerParams(
            collective_id=0, has_side_effects=True, vmem_limit_bytes=56 * 2**20
        ),
    )(owners, inputs, grads_out)


def solution(mesh):
    in_specs = (P(("group", "frame"), None), P(("group", "frame"), None), P("group"))
    out_specs = (P("group", None, None), P(("group", "frame"), None))
    fused = mesh.shape["frame"] == 16
    return jax.shard_map(
        body if fused else body_general,
        mesh=mesh,
        in_specs=in_specs,
        out_specs=out_specs,
        check_vma=False,
    )
```

```python
import functools

import jax
import jax.numpy as jnp
from jax import lax
from jax.experimental import pallas as pl
from jax.experimental.pallas import tpu as pltpu
from jax.sharding import PartitionSpec as P

BLOCK = 512
ITERS = 3


damping = 0.1


def partner_2(value, axis, stride):
    mask = 2**stride
    pairs = [(source, source ^ mask) for source in range(lax.axis_size(axis))]
    return lax.ppermute(value, axis, pairs)


def exact_dot(first_op, second_op):
    return jnp.dot(
        first_op, second_op, precision=lax.Precision.HIGHEST, preferred_element_type=jnp.float32
    )


def joined(own_part, other_part, own_first):
    return jnp.where(
        own_first,
        jnp.concatenate([own_part, other_part], 0),
        jnp.concatenate([other_part, own_part], 0),
    )


def body_general(inputs, grads_out, owners):
    frames = lax.axis_size("frame")
    blocks = frames // 4
    block_width = BLOCK
    quarter = block_width // 4
    half_rows = block_width // 2
    device_index = lax.axis_index("frame")
    quad_role = device_index % 4
    factor_side = quad_role // 2
    half_side = quad_role % 2
    token_scale = (inputs.shape[0] * frames) ** (-0.5)
    positions = jnp.arange(blocks, dtype=jnp.int32)
    inverse = jnp.sum(
        jnp.where(owners[None, :] == positions[:, None], positions[None, :], 0), axis=1
    )

    def block_product(block_id, row_offset, row_count):
        x_cols = lax.dynamic_slice_in_dim(
            inputs, block_id % 2 * block_width + row_offset, row_count, 1
        )
        y_cols = lax.dynamic_slice_in_dim(grads_out, block_id // 2 * block_width, block_width, 1)
        return (
            jnp.einsum("tk,tc->kc", x_cols, y_cols, preferred_element_type=jnp.float32)
            * token_scale
        )

    def one_slot(offset):
        return block_product(inverse[offset], 0, block_width)

    stacked = lax.map(
        one_slot, jnp.arange(lax.axis_size("frame") * quarter // block_width, dtype=jnp.int32)
    )
    own_part = lax.psum_scatter(
        stacked.reshape(lax.axis_size("frame") * quarter, block_width),
        "frame",
        scatter_dimension=0,
        tiled=True,
    )
    partner = partner_2(own_part, "frame", 0)
    pair_rows = joined(own_part, partner, half_side == 0)
    across = partner_2(pair_rows, "frame", 1)
    gradient = joined(pair_rows, across, factor_side == 0)
    operand = jnp.where(factor_side == 0, gradient, gradient.T)
    statistic = exact_dot(operand, operand.T) / block_width
    identity = jnp.eye(block_width, dtype=jnp.float32)
    damped = statistic + damping * jnp.trace(statistic) / block_width * identity
    frob_norm = jnp.sqrt(jnp.sum(damped * damped))
    zeta_scale = 5.0 / (2.0 * frob_norm)
    matrix = zeta_scale * damped
    root_full = zeta_scale**0.25 * identity
    for iteration in range(ITERS):
        factor_step = (5.0 * identity - matrix) * 0.25
        root_full = exact_dot(root_full, factor_step)
        square = exact_dot(factor_step, factor_step)
        matrix = exact_dot(exact_dot(square, square), matrix)
    roots_rows = lax.dynamic_slice_in_dim(root_full, half_side * half_rows, half_rows, 0)
    root_peer = partner_2(root_full, "frame", 1)
    left_root = jnp.where(factor_side == 0, root_full, root_peer)
    right_root = jnp.where(factor_side == 0, root_peer, root_full)
    left_rows = lax.dynamic_slice_in_dim(left_root, quad_role * quarter, quarter, 0)
    precond_rows = exact_dot(exact_dot(left_rows, gradient), right_root).astype(jnp.bfloat16)
    gathered = lax.all_gather(precond_rows, "frame", axis=0, tiled=True)
    gathered = gathered.reshape(blocks, block_width, block_width)
    precond = jnp.take(gathered, owners, axis=0)
    return (precond, roots_rows)


def halves(value):
    high = value.astype(jnp.bfloat16)
    low = (value - high.astype(jnp.float32)).astype(jnp.bfloat16)
    return high, low


def dot_halves(first, second, dims=((1,), (0,))):
    def one(a, b):
        return lax.dot_general(a, b, (dims, ((), ())), preferred_element_type=jnp.float32)

    return one(first[0], second[0]) + (one(first[0], second[1]) + one(first[1], second[0]))


def inverse_root(operand):
    size = operand.shape[0]
    parts = halves(operand)
    statistic = dot_halves(parts, parts, ((1,), (1,))) / size
    row = lax.broadcasted_iota(jnp.int32, (size, size), 0)
    col = lax.broadcasted_iota(jnp.int32, (size, size), 1)
    diagonal = row == col
    trace = jnp.sum(jnp.where(diagonal, statistic, 0.0))
    damped = statistic + jnp.where(diagonal, damping * trace / size, 0.0)
    zeta = 5.0 / (2.0 * jnp.sqrt(jnp.full((1, 1), jnp.sum(damped * damped), jnp.float32)))
    matrix = zeta * damped
    a = 1.25
    scale = 1.0
    deviation = None
    for iteration in range(ITERS):
        step = matrix * -0.25
        step_parts = halves(step)
        if deviation is None:
            deviation, scale = step, a
        else:
            deviation = scale * step + a * deviation + dot_halves(halves(deviation), step_parts)
            scale = scale * a
        if iteration < ITERS - 1:
            square = 2.0 * a * step + dot_halves(step_parts, step_parts)
            square_parts = halves(square)
            fourth = 2.0 * a * a * square + dot_halves(square_parts, square_parts)
            matrix = a**4 * matrix + dot_halves(halves(fourth), halves(matrix))
    root_scale = jnp.sqrt(jnp.sqrt(zeta))
    return root_scale * (deviation + jnp.where(diagonal, scale, 0.0))


def kernel(
    token_scale, owners_ref, x_ref, y_ref, out_ref, roots_ref,
    xt, part, from_core, y_sum, from_y, z_sum, from_z, grad, root_own, root_peer, rows_all,
    send_sem, recv_sem,
):
    me = lax.axis_index("frame")
    z, role = me // 4, me % 4
    y, core = role // 2, role % 2
    core_peer = me + 1 - 2 * core
    y_peer = me + 2 - 4 * y
    role_y = role + 2 - 4 * y
    planes = [((z + d) % 4) * 4 + role for d in range(4)]
    quarter, width = grad.shape[1], grad.shape[2]
    copies = []

    def copy(src, dst, target):
        index = len(copies)
        made = pltpu.make_async_remote_copy(
            src_ref=src,
            dst_ref=dst,
            send_sem=send_sem.at[index],
            recv_sem=recv_sem.at[index],
            device_id={"frame": target},
            device_id_type=pl.DeviceIdType.MESH,
        )
        made.start()
        copies.append(made)
        return made

    barrier = pltpu.get_barrier_semaphore()
    partners = [core_peer, y_peer] + planes[1:]
    for partner in partners:
        pl.semaphore_signal(
            barrier, inc=1, device_id={"frame": partner}, device_id_type=pl.DeviceIdType.MESH
        )

    half_width = width // 2
    for side in (1 - y, y):
        for bit in range(2):
            cols = pl.ds(pl.multiple_of(bit * width + side * half_width, half_width), half_width)
            xt[2 * bit + side] = x_ref[:, cols].T

    def compute(d, side):
        slot = slots[d]
        row_bit, col_bit = jnp.int32(0), jnp.int32(0)
        for b in range(1, 4):
            here = (owners_ref[b] == slot).astype(jnp.int32)
            row_bit, col_bit = row_bit + here * (b % 2), col_bit + here * (b // 2)
        x_rows = jnp.where(
            jnp.full((half_width, x_ref.shape[0]), row_bit) == 0, xt[side], xt[2 + side]
        )
        y_cols = jnp.where(
            jnp.full((x_ref.shape[0], width), col_bit) == 0, y_ref[:, :width], y_ref[:, width:]
        )
        product = jnp.dot(x_rows, y_cols, preferred_element_type=jnp.float32)
        part[d, 2 * side] = product[:quarter]
        part[d, 2 * side + 1] = product[quarter:]

    def to_core(d, side, index):
        return copy(part.at[d, 2 * side + 1 - core], from_core.at[d, index], core_peer)

    def to_y(d, sent):
        sent.wait_recv()
        y_sum[d] = part[d, 2 * (1 - y) + core] + from_core[d, 0]
        return copy(y_sum.at[d], from_y.at[d], y_peer)

    order = (0, 1, 2, 3)
    first, third = 3 * (1 - z // 2), 1 + z % 2
    slots = (first, 6 - first - third - z, third, z)
    away, kept, y_copies = {}, {}, {}
    for index, d in enumerate(order):
        compute(d, 1 - y)
        if index == 0:
            pl.semaphore_wait(barrier, len(partners))
        away[d] = to_core(d, 1 - y, 0)
        if index > 0:
            before = order[index - 1]
            y_copies[before] = to_y(before, away[before])
    y_copies[3] = to_y(3, away[3])
    for d in order:
        compute(d, y)
        kept[d] = to_core(d, y, 1)
    chain = send_sem.shape[0] - 8

    def z_copy(d, way):
        index = chain + 4 * way + slots[d]
        return pltpu.make_async_remote_copy(
            src_ref=z_sum.at[d],
            dst_ref=from_z.at[way, slots[d]],
            send_sem=send_sem.at[index],
            recv_sem=recv_sem.at[index],
            device_id={"frame": planes[1] if way == 0 else planes[3]},
            device_id_type=pl.DeviceIdType.MESH,
        )

    def add_arrived(d, way):
        @pl.when((z > 0) if way == 0 else (z < 3))
        def _():
            z_copy(d, way).wait_recv()
            z_sum[d] = z_sum[d] + from_z[way, slots[d]]

    for d in order:
        kept[d].wait_recv()
        y_copies[d].wait_recv()
        z_sum[d] = part[d, role] + from_core[d, 1] + from_y[d]
        if d < 3:
            @pl.when(slots[d] > z)
            def _():
                add_arrived(d, 0)
                z_copy(d, 0).start()

            @pl.when(slots[d] < z)
            def _():
                add_arrived(d, 1)
                z_copy(d, 1).start()

        else:
            add_arrived(d, 0)
            add_arrived(d, 1)
    total = z_sum[3]
    grad[role] = total * token_scale
    own_core = copy(grad.at[role], grad.at[role], core_peer)
    own_y = copy(grad.at[role], grad.at[role], y_peer)
    own_y.wait_recv()
    forward = copy(grad.at[role_y], grad.at[role_y], core_peer)
    own_core.wait_recv()
    forward.wait_recv()

    gradient = grad[...].reshape(4 * quarter, width)
    root_own[...] = inverse_root(jnp.where(core == 0, gradient, gradient.T))
    exchange = copy(root_own, root_peer, core_peer)
    exchange.wait_recv()

    half = pl.ds(pl.multiple_of(core * 2 * quarter, 2 * quarter), 2 * quarter)
    roots_ref[...] = jnp.where(y == core, root_own[half, :], root_peer[half, :])
    mine = pl.ds(pl.multiple_of(role * quarter, quarter), quarter)
    left = jnp.where(core == 0, root_own[mine, :], root_peer[mine, :])
    right = jnp.where(core == 0, root_peer[...], root_own[...])
    product = dot_halves(halves(left), halves(grad[...].reshape(4 * quarter, width)))
    rows_all[z, role] = dot_halves(halves(product), halves(right)).astype(jnp.bfloat16)

    base = len(copies)
    up, down, over, near, passed = base, base + 3, base + 6, base + 10, base + 14
    above, below = planes[1], planes[3]

    def rows_copy(index, plane, which, target):
        place = rows_all.at[plane, which]
        return pltpu.make_async_remote_copy(
            src_ref=place,
            dst_ref=place,
            send_sem=send_sem.at[index],
            recv_sem=recv_sem.at[index],
            device_id={"frame": target},
            device_id_type=pl.DeviceIdType.MESH,
        )

    def share(plane):
        rows_copy(over + plane, plane, role, y_peer).start()
        rows_copy(near + plane, plane, role, core_peer).start()

    def along(k):
        @pl.when(z >= k)
        def _():
            rows_copy(up + k - 1, z - k, role, above).wait_recv()
            if k < 3:
                @pl.when(z < 3)
                def _():
                    rows_copy(up + k, z - k, role, above).start()
            share(z - k)

        @pl.when(z + k <= 3)
        def _():
            rows_copy(down + k - 1, z + k, role, below).wait_recv()
            if k < 3:
                @pl.when(z > 0)
                def _():
                    rows_copy(down + k, z + k, role, below).start()
            share(z + k)

    def pass_on(plane):
        rows_copy(over + plane, plane, role, y_peer).wait_recv()
        rows_copy(passed + plane, plane, role_y, core_peer).start()

    def pass_step(k):
        @pl.when(z >= k)
        def _():
            pass_on(z - k)

        @pl.when(z + k <= 3)
        def _():
            pass_on(z + k)

    @pl.when(z < 3)
    def _():
        rows_copy(up, z, role, above).start()

    @pl.when(z > 0)
    def _():
        rows_copy(down, z, role, below).start()

    share(z)
    along(1)
    pass_on(z)
    along(2)
    pass_step(1)
    along(3)
    pass_step(2)
    pass_step(3)
    for plane in range(4):
        rows_copy(near + plane, plane, role, core_peer).wait_recv()
        rows_copy(passed + plane, plane, role_y, core_peer).wait_recv()
    for b in range(4):
        out_ref[b] = rows_all[owners_ref[b]].reshape(4 * quarter, width)
    for made in copies:
        made.wait_send()
    for d in range(3):
        @pl.when(slots[d] > z)
        def _():
            z_copy(d, 0).wait_send()

        @pl.when(slots[d] < z)
        def _():
            z_copy(d, 1).wait_send()

    for k in range(3):
        @pl.when((z >= k) & (z < 3))
        def _():
            rows_copy(up + k, z, role, above).wait_send()

        @pl.when((z + k <= 3) & (z > 0))
        def _():
            rows_copy(down + k, z, role, below).wait_send()

    for plane in range(4):
        rows_copy(over + plane, plane, role, y_peer).wait_send()
        rows_copy(near + plane, plane, role, core_peer).wait_send()
        rows_copy(passed + plane, plane, role_y, core_peer).wait_send()


def body(inputs, grads_out, owners):
    frames = lax.axis_size("frame")
    quarter = BLOCK // 4
    messages = 8 + 4 + 3 + 1 + 3 + 3 + 4 + 4 + 4 + 8
    f32 = jnp.float32
    return pl.pallas_call(
        functools.partial(kernel, (inputs.shape[0] * frames) ** (-0.5)),
        out_shape=(
            jax.ShapeDtypeStruct((4, BLOCK, BLOCK), jnp.bfloat16),
            jax.ShapeDtypeStruct((2 * quarter, BLOCK), f32),
        ),
        in_specs=[
            pl.BlockSpec(memory_space=pltpu.SMEM),
            pl.BlockSpec(memory_space=pltpu.VMEM),
            pl.BlockSpec(memory_space=pltpu.VMEM),
        ],
        out_specs=(
            pl.BlockSpec(memory_space=pltpu.VMEM),
            pl.BlockSpec(memory_space=pltpu.VMEM),
        ),
        scratch_shapes=[
            pltpu.VMEM((4, inputs.shape[1] // 4, inputs.shape[0]), jnp.bfloat16),
            pltpu.VMEM((4, 4, quarter, BLOCK), f32),
            pltpu.VMEM((4, 2, quarter, BLOCK), f32),
            pltpu.VMEM((4, quarter, BLOCK), f32),
            pltpu.VMEM((4, quarter, BLOCK), f32),
            pltpu.VMEM((4, quarter, BLOCK), f32),
            pltpu.VMEM((2, 4, quarter, BLOCK), f32),
            pltpu.VMEM((4, quarter, BLOCK), f32),
            pltpu.VMEM((BLOCK, BLOCK), f32),
            pltpu.VMEM((BLOCK, BLOCK), f32),
            pltpu.VMEM((4, 4, quarter, BLOCK), jnp.bfloat16),
            pltpu.SemaphoreType.DMA((messages,)),
            pltpu.SemaphoreType.DMA((messages,)),
        ],
        compiler_params=pltpu.CompilerParams(
            collective_id=0, has_side_effects=True, vmem_limit_bytes=56 * 2**20
        ),
    )(owners, inputs, grads_out)


def solution(mesh):
    in_specs = (P(("group", "frame"), None), P(("group", "frame"), None), P("group"))
    out_specs = (P("group", None, None), P(("group", "frame"), None))
    fused = mesh.shape["frame"] == 16
    return jax.shard_map(
        body if fused else body_general,
        mesh=mesh,
        in_specs=in_specs,
        out_specs=out_specs,
        check_vma=False,
    )
```

```python
import functools

import jax
import jax.numpy as jnp
from jax import lax
from jax.experimental import pallas as pl
from jax.experimental.pallas import tpu as pltpu
from jax.sharding import PartitionSpec as P

BLOCK = 512
ITERS = 3


damping = 0.1


def partner_2(value, axis, stride):
    mask = 2**stride
    pairs = [(source, source ^ mask) for source in range(lax.axis_size(axis))]
    return lax.ppermute(value, axis, pairs)


def exact_dot(first_op, second_op):
    return jnp.dot(
        first_op, second_op, precision=lax.Precision.HIGHEST, preferred_element_type=jnp.float32
    )


def joined(own_part, other_part, own_first):
    return jnp.where(
        own_first,
        jnp.concatenate([own_part, other_part], 0),
        jnp.concatenate([other_part, own_part], 0),
    )


def body_general(inputs, grads_out, owners):
    frames = lax.axis_size("frame")
    blocks = frames // 4
    block_width = BLOCK
    quarter = block_width // 4
    half_rows = block_width // 2
    device_index = lax.axis_index("frame")
    quad_role = device_index % 4
    factor_side = quad_role // 2
    half_side = quad_role % 2
    token_scale = (inputs.shape[0] * frames) ** (-0.5)
    positions = jnp.arange(blocks, dtype=jnp.int32)
    inverse = jnp.sum(
        jnp.where(owners[None, :] == positions[:, None], positions[None, :], 0), axis=1
    )

    def block_product(block_id, row_offset, row_count):
        x_cols = lax.dynamic_slice_in_dim(
            inputs, block_id % 2 * block_width + row_offset, row_count, 1
        )
        y_cols = lax.dynamic_slice_in_dim(grads_out, block_id // 2 * block_width, block_width, 1)
        return (
            jnp.einsum("tk,tc->kc", x_cols, y_cols, preferred_element_type=jnp.float32)
            * token_scale
        )

    def one_slot(offset):
        return block_product(inverse[offset], 0, block_width)

    stacked = lax.map(
        one_slot, jnp.arange(lax.axis_size("frame") * quarter // block_width, dtype=jnp.int32)
    )
    own_part = lax.psum_scatter(
        stacked.reshape(lax.axis_size("frame") * quarter, block_width),
        "frame",
        scatter_dimension=0,
        tiled=True,
    )
    partner = partner_2(own_part, "frame", 0)
    pair_rows = joined(own_part, partner, half_side == 0)
    across = partner_2(pair_rows, "frame", 1)
    gradient = joined(pair_rows, across, factor_side == 0)
    operand = jnp.where(factor_side == 0, gradient, gradient.T)
    statistic = exact_dot(operand, operand.T) / block_width
    identity = jnp.eye(block_width, dtype=jnp.float32)
    damped = statistic + damping * jnp.trace(statistic) / block_width * identity
    frob_norm = jnp.sqrt(jnp.sum(damped * damped))
    zeta_scale = 5.0 / (2.0 * frob_norm)
    matrix = zeta_scale * damped
    root_full = zeta_scale**0.25 * identity
    for iteration in range(ITERS):
        factor_step = (5.0 * identity - matrix) * 0.25
        root_full = exact_dot(root_full, factor_step)
        square = exact_dot(factor_step, factor_step)
        matrix = exact_dot(exact_dot(square, square), matrix)
    roots_rows = lax.dynamic_slice_in_dim(root_full, half_side * half_rows, half_rows, 0)
    root_peer = partner_2(root_full, "frame", 1)
    left_root = jnp.where(factor_side == 0, root_full, root_peer)
    right_root = jnp.where(factor_side == 0, root_peer, root_full)
    left_rows = lax.dynamic_slice_in_dim(left_root, quad_role * quarter, quarter, 0)
    precond_rows = exact_dot(exact_dot(left_rows, gradient), right_root).astype(jnp.bfloat16)
    gathered = lax.all_gather(precond_rows, "frame", axis=0, tiled=True)
    gathered = gathered.reshape(blocks, block_width, block_width)
    precond = jnp.take(gathered, owners, axis=0)
    return (precond, roots_rows)


def halves(value):
    high = value.astype(jnp.bfloat16)
    low = (value - high.astype(jnp.float32)).astype(jnp.bfloat16)
    return high, low


def dot_halves(first, second, dims=((1,), (0,))):
    def one(a, b):
        return lax.dot_general(a, b, (dims, ((), ())), preferred_element_type=jnp.float32)

    return one(first[0], second[0]) + (one(first[0], second[1]) + one(first[1], second[0]))


def inverse_root(operand):
    size = operand.shape[0]
    parts = halves(operand)
    statistic = dot_halves(parts, parts, ((1,), (1,))) / size
    row = lax.broadcasted_iota(jnp.int32, (size, size), 0)
    col = lax.broadcasted_iota(jnp.int32, (size, size), 1)
    diagonal = row == col
    trace = jnp.sum(jnp.where(diagonal, statistic, 0.0))
    damped = statistic + jnp.where(diagonal, damping * trace / size, 0.0)
    zeta = 5.0 / (2.0 * jnp.sqrt(jnp.full((1, 1), jnp.sum(damped * damped), jnp.float32)))
    matrix = zeta * damped
    a = 1.25
    scale = 1.0
    deviation = None
    for iteration in range(ITERS):
        step = matrix * -0.25
        step_parts = halves(step)
        if deviation is None:
            deviation, scale = step, a
        else:
            deviation = scale * step + a * deviation + dot_halves(halves(deviation), step_parts)
            scale = scale * a
        if iteration < ITERS - 1:
            square = 2.0 * a * step + dot_halves(step_parts, step_parts)
            square_parts = halves(square)
            fourth = 2.0 * a * a * square + dot_halves(square_parts, square_parts)
            matrix = a**4 * matrix + dot_halves(halves(fourth), halves(matrix))
    root_scale = jnp.sqrt(jnp.sqrt(zeta))
    return root_scale * (deviation + jnp.where(diagonal, scale, 0.0))


def kernel(
    token_scale, owners_ref, x_ref, y_ref, out_ref, roots_ref,
    xt, part, from_core, y_sum, from_y, z_sum, from_z, grad, root_own, root_peer, rows_all,
    send_sem, recv_sem,
):
    me = lax.axis_index("frame")
    z, role = me // 4, me % 4
    y, core = role // 2, role % 2
    core_peer = me + 1 - 2 * core
    y_peer = me + 2 - 4 * y
    role_y = role + 2 - 4 * y
    planes = [((z + d) % 4) * 4 + role for d in range(4)]
    quarter, width = grad.shape[1], grad.shape[2]
    copies = []

    def copy(src, dst, target):
        index = len(copies)
        made = pltpu.make_async_remote_copy(
            src_ref=src,
            dst_ref=dst,
            send_sem=send_sem.at[index],
            recv_sem=recv_sem.at[index],
            device_id={"frame": target},
            device_id_type=pl.DeviceIdType.MESH,
        )
        made.start()
        copies.append(made)
        return made

    barrier = pltpu.get_barrier_semaphore()
    partners = [core_peer, y_peer] + planes[1:]
    for partner in partners:
        pl.semaphore_signal(
            barrier, inc=1, device_id={"frame": partner}, device_id_type=pl.DeviceIdType.MESH
        )

    half_width = width // 2

    def turn(side):
        for bit in range(2):
            cols = pl.ds(pl.multiple_of(bit * width + side * half_width, half_width), half_width)
            xt[2 * bit + side] = x_ref[:, cols].T

    turn(1 - y)

    def compute(d, side):
        slot = slots[d]
        row_bit, col_bit = jnp.int32(0), jnp.int32(0)
        for b in range(1, 4):
            here = (owners_ref[b] == slot).astype(jnp.int32)
            row_bit, col_bit = row_bit + here * (b % 2), col_bit + here * (b // 2)
        x_rows = jnp.where(
            jnp.full((half_width, x_ref.shape[0]), row_bit) == 0, xt[side], xt[2 + side]
        )
        y_cols = jnp.where(
            jnp.full((x_ref.shape[0], width), col_bit) == 0, y_ref[:, :width], y_ref[:, width:]
        )
        product = jnp.dot(x_rows, y_cols, preferred_element_type=jnp.float32)
        part[d, 2 * side] = product[:quarter]
        part[d, 2 * side + 1] = product[quarter:]

    def to_core(d, side, index):
        return copy(part.at[d, 2 * side + 1 - core], from_core.at[d, index], core_peer)

    def to_y(d, sent):
        sent.wait_recv()
        y_sum[d] = part[d, 2 * (1 - y) + core] + from_core[d, 0]
        return copy(y_sum.at[d], from_y.at[d], y_peer)

    order = (0, 1, 2, 3)
    first, third = 3 * (1 - z // 2), 1 + z % 2
    slots = (first, 6 - first - third - z, third, z)
    away, kept, y_copies = {}, {}, {}
    for index, d in enumerate(order):
        compute(d, 1 - y)
        if index == 0:
            pl.semaphore_wait(barrier, len(partners))
        away[d] = to_core(d, 1 - y, 0)
        if index > 0:
            before = order[index - 1]
            y_copies[before] = to_y(before, away[before])
    y_copies[3] = to_y(3, away[3])
    turn(y)
    for d in order:
        compute(d, y)
        kept[d] = to_core(d, y, 1)
    chain = send_sem.shape[0] - 8

    def z_copy(d, way):
        index = chain + 4 * way + slots[d]
        return pltpu.make_async_remote_copy(
            src_ref=z_sum.at[d],
            dst_ref=from_z.at[way, slots[d]],
            send_sem=send_sem.at[index],
            recv_sem=recv_sem.at[index],
            device_id={"frame": planes[1] if way == 0 else planes[3]},
            device_id_type=pl.DeviceIdType.MESH,
        )

    def add_arrived(d, way):
        @pl.when((z > 0) if way == 0 else (z < 3))
        def _():
            z_copy(d, way).wait_recv()
            z_sum[d] = z_sum[d] + from_z[way, slots[d]]

    for d in order:
        kept[d].wait_recv()
        y_copies[d].wait_recv()
        z_sum[d] = part[d, role] + from_core[d, 1] + from_y[d]
        if d < 3:
            @pl.when(slots[d] > z)
            def _():
                add_arrived(d, 0)
                z_copy(d, 0).start()

            @pl.when(slots[d] < z)
            def _():
                add_arrived(d, 1)
                z_copy(d, 1).start()

        else:
            add_arrived(d, 0)
            add_arrived(d, 1)
    total = z_sum[3]
    grad[role] = total * token_scale
    own_core = copy(grad.at[role], grad.at[role], core_peer)
    own_y = copy(grad.at[role], grad.at[role], y_peer)
    own_y.wait_recv()
    forward = copy(grad.at[role_y], grad.at[role_y], core_peer)
    own_core.wait_recv()
    forward.wait_recv()

    gradient = grad[...].reshape(4 * quarter, width)
    root_own[...] = inverse_root(jnp.where(core == 0, gradient, gradient.T))
    exchange = copy(root_own, root_peer, core_peer)
    exchange.wait_recv()

    half = pl.ds(pl.multiple_of(core * 2 * quarter, 2 * quarter), 2 * quarter)
    roots_ref[...] = jnp.where(y == core, root_own[half, :], root_peer[half, :])
    mine = pl.ds(pl.multiple_of(role * quarter, quarter), quarter)
    left = jnp.where(core == 0, root_own[mine, :], root_peer[mine, :])
    right = jnp.where(core == 0, root_peer[...], root_own[...])
    product = dot_halves(halves(left), halves(grad[...].reshape(4 * quarter, width)))
    rows_all[z, role] = dot_halves(halves(product), halves(right)).astype(jnp.bfloat16)

    base = len(copies)
    piece = quarter // 2
    up, down, over, near, passed = base, base + 3, base + 6, base + 10, base + 14
    above, below = planes[1], planes[3]

    def rows_copy(number, plane, which, target, h):
        place = rows_all.at[plane, which, pl.ds(h * piece, piece)]
        index = base + 2 * (number - base) + h
        return pltpu.make_async_remote_copy(
            src_ref=place,
            dst_ref=place,
            send_sem=send_sem.at[index],
            recv_sem=recv_sem.at[index],
            device_id={"frame": target},
            device_id_type=pl.DeviceIdType.MESH,
        )

    def share(plane, h):
        rows_copy(over + plane, plane, role, y_peer, h).start()
        rows_copy(near + plane, plane, role, core_peer, h).start()

    def along(k, h):
        @pl.when(z >= k)
        def _():
            rows_copy(up + k - 1, z - k, role, above, h).wait_recv()
            if k < 3:
                @pl.when(z < 3)
                def _():
                    rows_copy(up + k, z - k, role, above, h).start()
            share(z - k, h)

        @pl.when(z + k <= 3)
        def _():
            rows_copy(down + k - 1, z + k, role, below, h).wait_recv()
            if k < 3:
                @pl.when(z > 0)
                def _():
                    rows_copy(down + k, z + k, role, below, h).start()
            share(z + k, h)

    def pass_on(plane, h):
        rows_copy(over + plane, plane, role, y_peer, h).wait_recv()
        rows_copy(passed + plane, plane, role_y, core_peer, h).start()

    def pass_step(k, h):
        @pl.when(z >= k)
        def _():
            pass_on(z - k, h)

        @pl.when(z + k <= 3)
        def _():
            pass_on(z + k, h)

    def begin(h):
        @pl.when(z < 3)
        def _():
            rows_copy(up, z, role, above, h).start()

        @pl.when(z > 0)
        def _():
            rows_copy(down, z, role, below, h).start()

        share(z, h)

    both = range(2)
    for h in both:
        begin(h)
    for h in both:
        along(1, h)
    for h in both:
        pass_on(z, h)
    for k in (2, 3):
        for h in both:
            along(k, h)
            pass_step(k - 1, h)
    for h in both:
        pass_step(3, h)
    for plane in range(4):
        for h in both:
            rows_copy(near + plane, plane, role, core_peer, h).wait_recv()
            rows_copy(passed + plane, plane, role_y, core_peer, h).wait_recv()
    for b in range(4):
        out_ref[b] = rows_all[owners_ref[b]].reshape(4 * quarter, width)
    for made in copies:
        made.wait_send()
    for d in range(3):
        @pl.when(slots[d] > z)
        def _():
            z_copy(d, 0).wait_send()

        @pl.when(slots[d] < z)
        def _():
            z_copy(d, 1).wait_send()

    for h in both:
        for k in range(3):
            @pl.when((z >= k) & (z < 3))
            def _():
                rows_copy(up + k, z, role, above, h).wait_send()

            @pl.when((z + k <= 3) & (z > 0))
            def _():
                rows_copy(down + k, z, role, below, h).wait_send()

        for plane in range(4):
            rows_copy(over + plane, plane, role, y_peer, h).wait_send()
            rows_copy(near + plane, plane, role, core_peer, h).wait_send()
            rows_copy(passed + plane, plane, role_y, core_peer, h).wait_send()


def body(inputs, grads_out, owners):
    frames = lax.axis_size("frame")
    quarter = BLOCK // 4
    messages = 8 + 4 + 3 + 1 + 2 * (3 + 3 + 4 + 4 + 4) + 8
    f32 = jnp.float32
    return pl.pallas_call(
        functools.partial(kernel, (inputs.shape[0] * frames) ** (-0.5)),
        out_shape=(
            jax.ShapeDtypeStruct((4, BLOCK, BLOCK), jnp.bfloat16),
            jax.ShapeDtypeStruct((2 * quarter, BLOCK), f32),
        ),
        in_specs=[
            pl.BlockSpec(memory_space=pltpu.SMEM),
            pl.BlockSpec(memory_space=pltpu.VMEM),
            pl.BlockSpec(memory_space=pltpu.VMEM),
        ],
        out_specs=(
            pl.BlockSpec(memory_space=pltpu.VMEM),
            pl.BlockSpec(memory_space=pltpu.VMEM),
        ),
        scratch_shapes=[
            pltpu.VMEM((4, inputs.shape[1] // 4, inputs.shape[0]), jnp.bfloat16),
            pltpu.VMEM((4, 4, quarter, BLOCK), f32),
            pltpu.VMEM((4, 2, quarter, BLOCK), f32),
            pltpu.VMEM((4, quarter, BLOCK), f32),
            pltpu.VMEM((4, quarter, BLOCK), f32),
            pltpu.VMEM((4, quarter, BLOCK), f32),
            pltpu.VMEM((2, 4, quarter, BLOCK), f32),
            pltpu.VMEM((4, quarter, BLOCK), f32),
            pltpu.VMEM((BLOCK, BLOCK), f32),
            pltpu.VMEM((BLOCK, BLOCK), f32),
            pltpu.VMEM((4, 4, quarter, BLOCK), jnp.bfloat16),
            pltpu.SemaphoreType.DMA((messages,)),
            pltpu.SemaphoreType.DMA((messages,)),
        ],
        compiler_params=pltpu.CompilerParams(
            collective_id=0, has_side_effects=True, vmem_limit_bytes=56 * 2**20
        ),
    )(owners, inputs, grads_out)


def solution(mesh):
    in_specs = (P(("group", "frame"), None), P(("group", "frame"), None), P("group"))
    out_specs = (P("group", None, None), P(("group", "frame"), None))
    fused = mesh.shape["frame"] == 16
    return jax.shard_map(
        body if fused else body_general,
        mesh=mesh,
        in_specs=in_specs,
        out_specs=out_specs,
        check_vma=False,
    )
```
